32 devices in a mesh: mode: 8 (over z, y), slab: 4 (over x, core).
Axes of the slice: x: 2, y: 2, z: 4, core: 2. Of those that a mesh axis runs over, the one named last changes fastest.
Arguments:
- adjoint: float32 [32, 2, 5, 65536], P('mode', None, None, 'slab'), may hold values from -6 to 6
- source: float32 [32, 2, 5, 65536], P('mode', None, None, 'slab'), may hold values from -6 to 6
- derivative: float32 [64, 64], replicated, may hold values from -0.75 to 0.75
- lift_matrix: float32 [64, 64], replicated, may hold values from -0.75 to 0.75
- jacobian: float32 [5, 5], replicated, may hold values from -2.5 to 2.5
- harmonics: float32 [5, 65536], P(None, 'slab'), may hold values from -6 to 6
- swirl_rate: float32 [65536], P('slab'), may hold values from -6 to 6
- coupling: float32 [32, 5, 2, 4], P('mode'), may hold values from -1 to 1
- mode_number: int32 [32], P('mode'), may hold values from -16 to 16, as said below
- partner: int32 [32], P('mode'), may hold values from 0 to 31, as said below
- upstream: int32 [1024], P('slab'), may hold values from 0 to 270, as said below
- face_list: int32 [64], P('slab'), may hold values from 0 to 255, as said below
Outputs:
- residual: float32 [32, 2, 5, 65536], P('mode', None, None, 'slab')
- sensitivity: float32 [32, 2, 5, 65536], P('mode', None, None, 'slab')
The draws below stay inside these ranges and needn't reach their ends.
Inputs may be any that keep to these rules, and one draw needn't show every extreme that they name: `mode_number`: never 0; every number from 1 to 16 appears once with each sign. partner[partner[m]] = m, mode_number[partner[m]] = -mode_number[m], and partner[m] lies in group (m // 4 + 16 // 4) mod (8). `upstream`: for the element at position e of its slab: below 16, the value is e, naming face e of the previous slab; otherwise the value minus 16 is a local element of the same slab before e. `face_list`: each block of 16 entries holds distinct local element numbers of its slab.
All inputs are finite; a program needn't handle non-finite values.
Results may differ from the reference program's by a relative error of at most 0.0001.
Values sent between devices are 32-bit elements; how exact they have to be, the bound alone decides.
A program may use at most 128 MiB of HBM per device.

```python
import jax
import jax.numpy as jnp
from jax import lax

NODES = 64
NV = 5
TAPS = 5
M_DEV = 4
ELEM_DEV = 256
FACE = 16
MODES = 32
HALF = 16
ELEMS = 1024
CELLS = 65536
N_MODE = 8
N_SLAB = 4


def mirror_tables(key):
    groups = MODES // M_DEV
    pairs = groups // 2
    first, second, third = jax.random.split(jax.random.fold_in(key, 7), 3)
    numbers = (jax.random.permutation(first, HALF) + 1).reshape(pairs, M_DEV).astype(jnp.int32)
    signs = (jax.random.randint(second, (pairs, M_DEV), 0, 2) * 2 - 1).astype(jnp.int32)
    orders = jax.vmap(lambda sub: jax.random.permutation(sub, M_DEV))(jax.random.split(third, pairs)).astype(jnp.int32)
    low_index = (jnp.arange(pairs, dtype=jnp.int32)[:, None] * M_DEV + jnp.arange(M_DEV, dtype=jnp.int32)[None, :]).reshape(-1)
    high_index = ((jnp.arange(pairs, dtype=jnp.int32)[:, None] + pairs) * M_DEV + orders).reshape(-1)
    values = (signs * numbers).reshape(-1)
    numbered = jnp.zeros((MODES,), jnp.int32).at[low_index].set(values).at[high_index].set(-values)
    paired = jnp.zeros((MODES,), jnp.int32).at[low_index].set(high_index).at[high_index].set(low_index)
    return (numbered, paired)


def draw_mode_number(key, part):
    return mirror_tables(key)[0]


def draw_partner(key, part):
    return mirror_tables(key)[1]


def draw_upstream(key, part):
    position = jnp.arange(ELEMS, dtype=jnp.int32) % ELEM_DEV
    back = jax.random.randint(jax.random.fold_in(key, 11), (ELEMS,), 0, 4).astype(jnp.int32)
    back = jnp.where(position == ELEM_DEV - 1, 0, back)
    local = position - 1 - jnp.minimum(back, jnp.maximum(position - 1, 0))
    return jnp.where(position < FACE, position, FACE + local).astype(jnp.int32)


def face_block(sub):
    first, second = jax.random.split(sub)
    middle = (jax.random.permutation(first, ELEM_DEV - 2)[:FACE - 2] + 1).astype(jnp.int32)
    ends = jnp.array([0, ELEM_DEV - 1], dtype=jnp.int32)
    block = jnp.concatenate([ends, middle])
    order = jax.random.permutation(second, FACE).astype(jnp.int32)
    return jnp.take(block, order)


def draw_face_list(key, part):
    subkeys = jax.random.split(jax.random.fold_in(key, 13), ELEMS // ELEM_DEV)
    rows = jax.vmap(face_block)(subkeys)
    return rows.reshape(-1).astype(jnp.int32)


def shard_levels(rng, extent, cuts, least, largest):
    level = 1.0
    for axis_at, parts in cuts:
        draws = jax.random.uniform(jax.random.fold_in(jax.random.fold_in(rng, 6), axis_at), (parts,), jnp.float32, least / len(cuts), largest / len(cuts))
        level = level * jnp.repeat(jnp.exp(draws), extent[axis_at] // parts).reshape((-1,) + (1,) * (len(extent) - 1 - axis_at))
    return level


def normal_values(rng, extent, scale, most, pieces=(), held_as=jnp.bfloat16):
    values = scale * jax.random.normal(rng, extent, jnp.float32)
    if pieces:
        values = values * shard_levels(rng, extent, pieces, -0.22, 0.18)
    return jnp.clip(values, -most, most).astype(held_as)


def setup_inputs(seed: int = 0) -> dict:
    keys = jax.random.split(jax.random.key(seed), 13)
    adjoint = normal_values(keys[0], (MODES, 2, NV, CELLS), 1.0, 6.0, ((0, 8), (3, 4)), jnp.float32)
    source = normal_values(keys[1], (MODES, 2, NV, CELLS), 1.0, 6.0, ((0, 8), (3, 4)), jnp.float32)
    derivative = normal_values(keys[2], (NODES, NODES), NODES ** -0.5, 0.75, (), jnp.float32)
    lift_matrix = normal_values(keys[3], (NODES, NODES), NODES ** -0.5, 0.75, (), jnp.float32)
    jacobian = normal_values(keys[4], (NV, NV), NV ** -0.5, 2.5, (), jnp.float32)
    harmonics = normal_values(keys[5], (TAPS, CELLS), 1.0, 6.0, ((1, 4),), jnp.float32)
    swirl_rate = normal_values(keys[6], (CELLS,), 1.0, 6.0, ((0, 4),), jnp.float32)
    coupling = normal_values(keys[7], (MODES, TAPS, 2, M_DEV), (2 * M_DEV * TAPS) ** -0.5, 1.0, ((0, 8),), jnp.float32)
    mode_number = draw_mode_number(jax.random.fold_in(keys[12], 71), 0)
    partner = draw_partner(jax.random.fold_in(keys[12], 71), 0)
    upstream = draw_upstream(jax.random.fold_in(keys[12], 71), 0)
    face_list = draw_face_list(jax.random.fold_in(keys[12], 71), 0)
    return dict(adjoint=adjoint, source=source, derivative=derivative, lift_matrix=lift_matrix, jacobian=jacobian, harmonics=harmonics, swirl_rate=swirl_rate, coupling=coupling, mode_number=mode_number, partner=partner, upstream=upstream, face_list=face_list)


def reference(adjoint, source, derivative, lift_matrix, jacobian, harmonics, swirl_rate, coupling, mode_number, partner, upstream, face_list):
    highest = lax.Precision.HIGHEST
    field = adjoint.reshape(MODES, 2, NV, N_SLAB, ELEM_DEV, NODES)
    face_rows = face_list.reshape(N_SLAB, FACE)
    up_rows = upstream.reshape(N_SLAB, ELEM_DEV)
    faces = jnp.stack([jnp.take(field[:, :, :, slab_id], face_rows[slab_id], axis=3) for slab_id in range(N_SLAB)], axis=3)
    halo = jnp.concatenate([jnp.zeros_like(faces[:, :, :, :1]), faces[:, :, :, :-1]], axis=3)
    extended = jnp.concatenate([halo, field], axis=4)
    upper = jnp.stack([jnp.take(extended[:, :, :, slab_id], up_rows[slab_id], axis=3) for slab_id in range(N_SLAB)], axis=3)
    meridional = jnp.einsum("mcvsej,ij->mcvsei", field, derivative, precision=highest)
    meridional = meridional + jnp.einsum("mcvsej,ij->mcvsei", upper, lift_matrix, precision=highest)
    meridional = meridional.reshape(MODES, 2, NV, CELLS)
    convective = jnp.einsum("wv,mcvx->mcwx", jacobian, meridional, precision=highest)
    factor = (mode_number.astype(jnp.float32) / HALF)[:, None, None] * swirl_rate[None, None, :]
    azimuthal = jnp.stack([-factor * adjoint[:, 1], factor * adjoint[:, 0]], axis=1)
    groups = adjoint.reshape(N_MODE, M_DEV, 2, NV, CELLS)
    weights = coupling.reshape(N_MODE, M_DEV, TAPS, 2, M_DEV)
    mixing = jnp.zeros((N_MODE, M_DEV, 2, NV, CELLS), jnp.float32)
    for tap in range(TAPS):
        rolled = jnp.roll(groups, tap - TAPS // 2, axis=0)
        real_w = weights[:, :, tap, 0]
        imag_w = weights[:, :, tap, 1]
        real_part = jnp.einsum("gab,gbvx->gavx", real_w, rolled[:, :, 0], precision=highest) - jnp.einsum("gab,gbvx->gavx", imag_w, rolled[:, :, 1], precision=highest)
        imag_part = jnp.einsum("gab,gbvx->gavx", real_w, rolled[:, :, 1], precision=highest) + jnp.einsum("gab,gbvx->gavx", imag_w, rolled[:, :, 0], precision=highest)
        mixing = mixing + jnp.stack([real_part, imag_part], axis=2) * harmonics[tap][None, None, None, None, :]
    mixing = mixing.reshape(MODES, 2, NV, CELLS)
    residual = source - convective - azimuthal - mixing
    opposite = jnp.take(residual, partner, axis=0)
    sensitivity = residual + jnp.stack([opposite[:, 0], -opposite[:, 1]], axis=1)
    return (residual, sensitivity)
```

```python
import jax
import jax.numpy as jnp
from jax import lax
from jax.experimental import pallas as pl
from jax.experimental.pallas import tpu as pltpu
from jax.sharding import PartitionSpec as P

TAPS = 5
BLOCK = 32
LANES = 128
MESH = pl.DeviceIdType.MESH


def split(x):
    high = x.astype(jnp.bfloat16)
    low = (x - high.astype(jnp.float32)).astype(jnp.bfloat16)
    return high, low


def dot(a, b):
    return jnp.dot(a, b, preferred_element_type=jnp.float32)


def times_i(x):
    even = lax.broadcasted_iota(jnp.int32, x.shape, 0) % 2 == 0
    return jnp.where(even, -pltpu.roll(x, x.shape[0] - 1, 0), pltpu.roll(x, 1, 0))


def doubled(x, half):
    low = lax.broadcasted_iota(jnp.int32, x.shape, 1) < LANES // 2
    other = pltpu.roll(x, LANES // 2, 1)
    return jnp.where(low, x, other) if half == 0 else jnp.where(low, other, x)


def by_half(x, y):
    return jnp.where(lax.broadcasted_iota(jnp.int32, x.shape, 1) < LANES // 2, x, y)


def kernel(
    coup,
    jac,
    fac,
    perm,
    adj,
    src,
    kmat,
    pick,
    pick_halo,
    harm,
    swirl,
    res,
    sens,
    near,
    opp,
    mer,
    faces,
    halo,
    send_sem,
    recv_sem,
    halo_sem,
):
    modes, nv, rows, _ = adj.shape
    frows = faces.shape[2]
    n_mode = lax.axis_size("mode")
    n_slab = lax.axis_size("slab")
    me = lax.axis_index("mode")
    slab = lax.axis_index("slab")
    odd = me % 2
    above = (me + 2) % n_mode
    below = (me + n_mode - 2) % n_mode
    pair = me + 1 - 2 * odd
    across = (me + n_mode // 2) % n_mode
    after = (slab + 1) % n_slab
    before = (slab + n_slab - 1) % n_slab

    barrier = pltpu.get_barrier_semaphore()
    for other in (above, below, pair, across):
        pl.semaphore_signal(barrier, inc=1, device_id=(other, slab), device_id_type=MESH)
    for other in (after, before):
        pl.semaphore_signal(barrier, inc=1, device_id=(me, other), device_id_type=MESH)
    pl.semaphore_wait(barrier, 6)

    def copy(kind, v, source, target, device):
        return pltpu.make_async_remote_copy(
            src_ref=source.at[:, v],
            dst_ref=target.at[:, v],
            send_sem=send_sem.at[kind, v],
            recv_sem=recv_sem.at[kind, v],
            device_id=(device, slab),
            device_id_type=MESH,
        )

    def up(v):
        return copy(0, v, adj, near.at[0], above)

    def down(v):
        return copy(1, v, adj, near.at[1], below)

    def beside(v):
        return copy(2, v, adj, near.at[2], pair)

    def onward(v):
        return copy(3, v, near.at[1 - odd], near.at[3], pair)

    def over(v):
        return copy(4, v, res, opp, across)

    @pl.loop(0, nv)
    def _(v):
        up(v).start()
        down(v).start()
        beside(v).start()

    @pl.loop(0, modes * nv)
    def _(i):
        m = i // nv
        v = i % nv
        k_high, k_low = split(kmat[...])
        x_high, x_low = split(adj[m, v])
        lifted = dot(x_high, k_high) + dot(x_low, k_high) + dot(x_high, k_low)
        tall = jnp.concatenate([lifted[:, LANES : 2 * LANES], lifted[:, 2 * LANES :]], axis=0)
        picked = dot(pick[...], jnp.concatenate(split(tall), axis=1))
        picked = picked[:, :LANES] + picked[:, LANES:]
        mer[m, v] = lifted[:, :LANES] + by_half(picked[:rows], picked[rows : 2 * rows])
        faces[m, v] = by_half(
            picked[2 * rows : 2 * rows + frows], picked[2 * rows + frows :]
        )

    halo_copy = pltpu.make_async_remote_copy(
        src_ref=faces,
        dst_ref=halo,
        send_sem=halo_sem.at[0],
        recv_sem=halo_sem.at[1],
        device_id=(me, after),
        device_id_type=MESH,
    )
    halo_copy.start()

    def mix(total, values, tap, r0):
        turned = [times_i(x) for x in values]
        amplitude = harm[tap, pl.ds(r0, BLOCK), :]
        out = []
        for a in range(modes):
            at = (a * TAPS + tap) * 2 * modes
            part = values[0] * coup[at] + turned[0] * coup[at + modes]
            for b in range(1, modes):
                part = part + values[b] * coup[at + b] + turned[b] * coup[at + modes + b]
            out.append(total[a] - part * amplitude)
        return out

    @pl.loop(0, nv)
    def _(v):
        @pl.loop(0, rows // BLOCK)
        def _(j):
            r0 = pl.multiple_of(j * BLOCK, BLOCK)
            values = [adj[b, v, pl.ds(r0, BLOCK), :] for b in range(modes)]
            rate = swirl[pl.ds(r0, BLOCK), :]
            total = [
                src[a, v, pl.ds(r0, BLOCK), :] - times_i(values[a]) * (rate * fac[a])
                for a in range(modes)
            ]
            total = mix(total, values, TAPS // 2, r0)
            for a in range(modes):
                res[a, v, pl.ds(r0, BLOCK), :] = total[a]

    halo_copy.wait()
    present = jnp.where(slab == 0, 0.0, 1.0)

    @pl.loop(0, modes * nv)
    def _(i):
        m = i // nv
        v = i % nv
        got = halo[m, v] * present
        tall = jnp.concatenate([doubled(got, 0), doubled(got, 1)], axis=0)
        picked = dot(pick_halo[...], jnp.concatenate(split(tall), axis=1))
        picked = picked[:, :LANES] + picked[:, LANES:]
        mer[m, v] = mer[m, v] + by_half(picked[:rows], picked[rows:])

    @pl.loop(0, modes)
    def _(m):
        @pl.loop(0, rows // BLOCK)
        def _(j):
            r0 = pl.multiple_of(j * BLOCK, BLOCK)
            values = [mer[m, v, pl.ds(r0, BLOCK), :] for v in range(nv)]
            for w in range(nv):
                part = values[0] * jac[w * nv]
                for v in range(1, nv):
                    part = part + values[v] * jac[w * nv + v]
                res[m, w, pl.ds(r0, BLOCK), :] = res[m, w, pl.ds(r0, BLOCK), :] - part

    def add_mix(v, slots):
        @pl.loop(0, rows // BLOCK)
        def _(j):
            r0 = pl.multiple_of(j * BLOCK, BLOCK)
            total = [res[a, v, pl.ds(r0, BLOCK), :] for a in range(modes)]
            for slot, tap in slots:
                values = [near[slot, b, v, pl.ds(r0, BLOCK), :] for b in range(modes)]
                total = mix(total, values, tap, r0)
            for a in range(modes):
                res[a, v, pl.ds(r0, BLOCK), :] = total[a]

    @pl.loop(0, nv)
    def _(v):
        up(v).wait_recv()
        down(v).wait_recv()
        onward(v).start()
        beside(v).wait_recv()
        add_mix(v, ((0, 4), (1, 0), (2, 1 + 2 * odd)))
        onward(v).wait_recv()
        add_mix(v, ((3, 3 - 2 * odd),))
        over(v).start()

    @pl.loop(0, nv)
    def _(v):
        over(v).wait_recv()

        @pl.loop(0, rows // BLOCK)
        def _(j):
            r0 = pl.multiple_of(j * BLOCK, BLOCK)
            even = lax.broadcasted_iota(jnp.int32, (BLOCK, LANES), 0) % 2 == 0
            values = [opp[b, v, pl.ds(r0, BLOCK), :] for b in range(modes)]
            values = [jnp.where(even, x, -x) for x in values]
            for a in range(modes):
                total = res[a, v, pl.ds(r0, BLOCK), :]
                for b in range(modes):
                    total = total + values[b] * perm[a * modes + b]
                sens[a, v, pl.ds(r0, BLOCK), :] = total

    @pl.loop(0, nv)
    def _(v):
        up(v).wait_send()
        down(v).wait_send()
        beside(v).wait_send()
        onward(v).wait_send()
        over(v).wait_send()


def per_device(
    adjoint,
    source,
    derivative,
    lift_matrix,
    jacobian,
    harmonics,
    swirl_rate,
    coupling,
    mode_number,
    partner,
    upstream,
    face_list,
):
    modes, _, nv, cells = adjoint.shape
    nodes = derivative.shape[0]
    elements = cells // nodes
    face_count = face_list.shape[0]
    tiles = cells // LANES
    rows = 2 * tiles
    frows = face_count
    highest_mode = modes * lax.axis_size("mode") // 2

    def to_rows(x):
        x = x.reshape(modes, 2, nv, tiles, LANES)
        return x.transpose(0, 2, 3, 1, 4).reshape(modes, nv, rows, LANES)

    def from_rows(x):
        x = x.reshape(modes, nv, tiles, 2, LANES)
        return x.transpose(0, 3, 1, 2, 4).reshape(modes, 2, nv, cells)

    eye = jnp.eye(2, dtype=jnp.float32)
    lift = lift_matrix.T
    nothing = jnp.zeros_like(lift)
    kmat = jnp.concatenate(
        [
            jnp.kron(eye, derivative.T),
            jnp.block([[lift, lift], [nothing, nothing]]),
            jnp.block([[nothing, nothing], [lift, lift]]),
        ],
        axis=1,
    )

    def spread(values):
        values = values.reshape(-1, 2).T
        return jnp.repeat(values.reshape(-1), 2)

    def match(wanted, held):
        part = jnp.arange(wanted.shape[0]) % 2
        part_held = jnp.arange(held.shape[0]) % 2
        same = (wanted[:, None] == held[None, :]) & (part[:, None] == part_held[None, :])
        return same.astype(jnp.bfloat16)

    element = spread(jnp.arange(elements, dtype=jnp.int32))
    face = spread(jnp.arange(face_count, dtype=jnp.int32))
    wanted = spread(upstream)
    pick = match(
        jnp.concatenate([wanted - face_count, spread(face_list)]), element
    )
    pick_halo = match(wanted, face)
    harm = jnp.repeat(harmonics.reshape(TAPS, tiles, LANES), 2, axis=1)
    swirl = jnp.repeat(swirl_rate.reshape(tiles, LANES), 2, axis=0)
    factor = mode_number.astype(jnp.float32) / highest_mode
    perm = (partner[:, None] % modes == jnp.arange(modes)[None, :]).astype(jnp.float32)

    panel = (modes, nv, rows, LANES)
    small = (modes, nv, frows, LANES)
    smem = pl.BlockSpec(memory_space=pltpu.SMEM)
    vmem = pl.BlockSpec(memory_space=pltpu.VMEM)
    residual, sensitivity = pl.pallas_call(
        kernel,
        out_shape=[jax.ShapeDtypeStruct(panel, jnp.float32)] * 2,
        in_specs=[smem] * 4 + [vmem] * 7,
        out_specs=[vmem] * 2,
        scratch_shapes=[
            pltpu.VMEM((4,) + panel, jnp.float32),
            pltpu.VMEM(panel, jnp.float32),
            pltpu.VMEM(panel, jnp.float32),
            pltpu.VMEM(small, jnp.float32),
            pltpu.VMEM(small, jnp.float32),
            pltpu.SemaphoreType.DMA((5, nv)),
            pltpu.SemaphoreType.DMA((5, nv)),
            pltpu.SemaphoreType.DMA((2,)),
        ],
        compiler_params=pltpu.CompilerParams(
            collective_id=0, has_side_effects=True, vmem_limit_bytes=48 * 1024 * 1024
        ),
    )(
        coupling.reshape(-1),
        jacobian.reshape(-1),
        factor,
        perm.reshape(-1),
        to_rows(adjoint),
        to_rows(source),
        kmat,
        pick,
        pick_halo,
        harm,
        swirl,
    )
    return (from_rows(residual), from_rows(sensitivity))


def solution(mesh):
    in_specs = (
        P("mode", None, None, "slab"),
        P("mode", None, None, "slab"),
        P(),
        P(),
        P(),
        P(None, "slab"),
        P("slab"),
        P("mode", None, None, None),
        P("mode"),
        P("mode"),
        P("slab"),
        P("slab"),
    )
    out_specs = (P("mode", None, None, "slab"), P("mode", None, None, "slab"))
    return jax.shard_map(
        per_device, mesh=mesh, in_specs=in_specs, out_specs=out_specs, check_vma=False
    )
```

```python
import jax
import jax.numpy as jnp
from jax import lax
from jax.experimental import pallas as pl
from jax.experimental.pallas import tpu as pltpu
from jax.sharding import PartitionSpec as P

TAPS = 5
BLOCK = 32
LANES = 128
WINDOW = 3
MESH = pl.DeviceIdType.MESH


def split(x):
    high = x.astype(jnp.bfloat16)
    low = (x - high.astype(jnp.float32)).astype(jnp.bfloat16)
    return high, low


def dot(a, b):
    return jnp.dot(a, b, preferred_element_type=jnp.float32)


def dot_t(a, b):
    return lax.dot_general(a, b, (((1,), (1,)), ((), ())), preferred_element_type=jnp.float32)


def times_i(x):
    even = lax.broadcasted_iota(jnp.int32, x.shape, 0) % 2 == 0
    return jnp.where(even, -pltpu.roll(x, x.shape[0] - 1, 0), pltpu.roll(x, 1, 0))


def doubled(x, half):
    low = lax.broadcasted_iota(jnp.int32, x.shape, 1) < LANES // 2
    other = pltpu.roll(x, LANES // 2, 1)
    return jnp.where(low, x, other) if half == 0 else jnp.where(low, other, x)


def by_half(x, y):
    return jnp.where(lax.broadcasted_iota(jnp.int32, x.shape, 1) < LANES // 2, x, y)


def spot(i, span):
    return (i % span) // 2 * 2 + i // span


def kernel(
    coup,
    jac,
    number,
    partner,
    adj_hbm,
    src_hbm,
    derivative,
    lift,
    upstream,
    face_list,
    harm_in,
    swirl_in,
    res,
    sens,
    adj,
    src,
    near,
    opp,
    mer,
    faces,
    halo,
    kmat,
    pick,
    pick_halo,
    harm,
    swirl,
    send_sem,
    recv_sem,
    halo_sem,
    load_sem,
):
    modes, nv, rows, _ = adj.shape
    chunks = 2 * nv
    part = rows // 2
    frows = faces.shape[2]
    n_mode = lax.axis_size("mode")
    n_slab = lax.axis_size("slab")
    me = lax.axis_index("mode")
    slab = lax.axis_index("slab")
    odd = me % 2
    above = (me + 2) % n_mode
    below = (me + n_mode - 2) % n_mode
    pair = me + 1 - 2 * odd
    across = (me + n_mode // 2) % n_mode
    after = (slab + 1) % n_slab
    before = (slab + n_slab - 1) % n_slab

    load_adj = pltpu.make_async_copy(adj_hbm, adj, load_sem.at[0])
    load_src = pltpu.make_async_copy(src_hbm, src, load_sem.at[1])
    load_adj.start()
    load_src.start()

    barrier = pltpu.get_barrier_semaphore()
    for other in (above, below, pair, across):
        pl.semaphore_signal(barrier, inc=1, device_id=(other, slab), device_id_type=MESH)
    for other in (after, before):
        pl.semaphore_signal(barrier, inc=1, device_id=(me, other), device_id_type=MESH)
    pl.semaphore_wait(barrier, 6)
    load_adj.wait()

    def place(q):
        return q // 2, pl.multiple_of(q % 2 * part, part)

    def copy(kind, q, source, target, device):
        v, r0 = place(q)
        return pltpu.make_async_remote_copy(
            src_ref=source.at[:, v, pl.ds(r0, part)],
            dst_ref=target.at[:, v, pl.ds(r0, part)],
            send_sem=send_sem.at[kind, q],
            recv_sem=recv_sem.at[kind, q],
            device_id=(device, slab),
            device_id_type=MESH,
        )

    def up(q):
        return copy(0, q, adj, near.at[0], above)

    def down(q):
        return copy(1, q, adj, near.at[1], below)

    def beside(q):
        return copy(2, q, adj, near.at[2], pair)

    def onward(q):
        return copy(3, q, near.at[1 - odd], near.at[3], pair)

    def over(q):
        return copy(4, q, res, opp, across)

    def begin(q):
        up(q).start()
        down(q).start()
        beside(q).start()

    @pl.loop(0, WINDOW)
    def _(q):
        begin(q)

    def arrive(q):
        up(q).wait_send()
        down(q).wait_send()

        @pl.when(q + WINDOW < chunks)
        def _():
            begin(q + WINDOW)

        up(q).wait_recv()
        down(q).wait_recv()
        onward(q).start()
        beside(q).wait_recv()

    span = rows
    d = derivative[...]
    low = lift[...]
    none = jnp.zeros_like(d)
    kmat[...] = jnp.concatenate(
        [
            jnp.concatenate([d, none], axis=1),
            jnp.concatenate([none, d], axis=1),
            jnp.concatenate([low, none], axis=1),
            jnp.concatenate([low, none], axis=1),
            jnp.concatenate([none, low], axis=1),
            jnp.concatenate([none, low], axis=1),
        ],
        axis=0,
    )

    def iota(shape, axis):
        return lax.broadcasted_iota(jnp.int32, shape, axis)

    def wanted_rows(values, count, span_out):
        held = values.shape[1]
        mine = spot(iota((count, held), 0), span_out)
        chosen = jnp.where(mine == iota((count, held), 1), values, 0.0)
        return jnp.sum(chosen, axis=1, keepdims=True)

    def one_hot(wanted, count, width, span_in):
        held = spot(iota((count, width), 1), span_in).astype(jnp.float32)
        same = (iota((count, width), 0) % 2) == (iota((count, width), 1) % 2)
        hot = jnp.where(wanted == held, 1.0, 0.0)
        return jnp.where(same, hot, 0.0).astype(jnp.bfloat16)

    source_row = wanted_rows(upstream[...].astype(jnp.float32), 2 * rows, span)
    face_row = wanted_rows(face_list[...].astype(jnp.float32), 2 * frows, frows)
    pick[: 2 * rows] = one_hot(source_row - float(frows), 2 * rows, 2 * rows, span)
    pick[2 * rows :] = one_hot(face_row, 2 * frows, 2 * rows, span)
    pick_halo[...] = one_hot(source_row, 2 * rows, 2 * frows, frows)

    twice = jnp.where(
        iota((rows, rows // 2), 0) // 2 == iota((rows, rows // 2), 1), 1.0, 0.0
    ).astype(jnp.bfloat16)

    def double(x):
        high = x.astype(jnp.bfloat16)
        rest, last = split(x - high.astype(jnp.float32))
        return dot(twice, high) + dot(twice, rest) + dot(twice, last)

    for tap in range(TAPS):
        harm[tap] = double(harm_in[:, tap, :])
    swirl[...] = double(swirl_in[...])
    load_src.wait()

    half_modes = float(modes * n_mode // 2)
    fac = [number[a].astype(jnp.float32) / half_modes for a in range(modes)]

    def gather(i):
        m = i // nv
        v = i % nv
        k_high, k_low = split(kmat[...])
        x_high, x_low = split(adj[m, v])
        lifted = dot_t(x_high, k_high) + dot_t(x_low, k_high) + dot_t(x_high, k_low)
        tall = jnp.concatenate([lifted[:, LANES : 2 * LANES], lifted[:, 2 * LANES :]], axis=0)
        picked = dot(pick[...], jnp.concatenate(split(tall), axis=1))
        picked = picked[:, :LANES] + picked[:, LANES:]
        mer[m, v] = lifted[:, :LANES] + by_half(picked[:rows], picked[rows : 2 * rows])
        faces[m, v] = by_half(
            picked[2 * rows : 2 * rows + frows], picked[2 * rows + frows :]
        )

    halo_copy = pltpu.make_async_remote_copy(
        src_ref=faces,
        dst_ref=halo,
        send_sem=halo_sem.at[0],
        recv_sem=halo_sem.at[1],
        device_id=(me, after),
        device_id_type=MESH,
    )

    def mix(total, values, tap, r0):
        turned = [times_i(x) for x in values]
        amplitude = harm[tap, pl.ds(r0, BLOCK), :]
        out = []
        for a in range(modes):
            at = a * 2 * modes
            term = values[0] * coup[at, tap] + turned[0] * coup[at + modes, tap]
            for b in range(1, modes):
                term = term + values[b] * coup[at + b, tap]
                term = term + turned[b] * coup[at + modes + b, tap]
            out.append(total[a] - term * amplitude)
        return out

    def direct(q):
        v, start = place(q)

        @pl.loop(0, part // BLOCK)
        def _(j):
            r0 = pl.multiple_of(start + j * BLOCK, BLOCK)
            values = [adj[b, v, pl.ds(r0, BLOCK), :] for b in range(modes)]
            rate = swirl[pl.ds(r0, BLOCK), :]
            total = [
                src[a, v, pl.ds(r0, BLOCK), :] - times_i(values[a]) * (rate * fac[a])
                for a in range(modes)
            ]
            total = mix(total, values, TAPS // 2, r0)
            for slot, tap in ((0, 4), (1, 0), (2, 1 + 2 * odd)):
                values = [near[slot, b, v, pl.ds(r0, BLOCK), :] for b in range(modes)]
                total = mix(total, values, tap, r0)
            for a in range(modes):
                res[a, v, pl.ds(r0, BLOCK), :] = total[a]

    def finish(q):
        onward(q).wait_recv()
        v, start = place(q)

        @pl.loop(0, part // BLOCK)
        def _(j):
            r0 = pl.multiple_of(start + j * BLOCK, BLOCK)
            total = []
            for a in range(modes):
                term = res[a, v, pl.ds(r0, BLOCK), :]
                for w in range(nv):
                    term = term - mer[a, w, pl.ds(r0, BLOCK), :] * jac[v, w]
                total.append(term)
            values = [near[3, b, v, pl.ds(r0, BLOCK), :] for b in range(modes)]
            total = mix(total, values, 3 - 2 * odd, r0)
            for a in range(modes):
                res[a, v, pl.ds(r0, BLOCK), :] = total[a]

    @pl.loop(0, nv)
    def _(q):
        @pl.loop(q * modes, (q + 1) * modes)
        def _(i):
            gather(i)

        arrive(q)
        direct(q)

    halo_copy.start()

    @pl.loop(nv, nv + 1)
    def _(q):
        arrive(q)
        direct(q)

    halo_copy.wait()
    present = jnp.where(slab == 0, 0.0, 1.0)

    @pl.loop(0, modes * nv)
    def _(i):
        m = i // nv
        v = i % nv
        got = halo[m, v] * present
        tall = jnp.concatenate([doubled(got, 0), doubled(got, 1)], axis=0)
        picked = dot(pick_halo[...], jnp.concatenate(split(tall), axis=1))
        picked = picked[:, :LANES] + picked[:, LANES:]
        mer[m, v] = mer[m, v] + by_half(picked[:rows], picked[rows:])

    @pl.loop(nv + 1, chunks)
    def _(q):
        @pl.when(q == chunks - 1)
        def _():
            over(0).start()

        arrive(q)
        direct(q)

        @pl.loop(2 * (q - nv - 1), 2 * (q - nv))
        def _(c):
            finish(c)

    @pl.loop(1, WINDOW)
    def _(q):
        over(q).start()

    @pl.loop(2 * (nv - 1), chunks)
    def _(q):
        finish(q)

    @pl.loop(0, chunks)
    def _(q):
        over(q).wait_send()

        @pl.when(q + WINDOW < chunks)
        def _():
            over(q + WINDOW).start()

        over(q).wait_recv()
        v, start = place(q)

        @pl.loop(0, part // BLOCK)
        def _(j):
            r0 = pl.multiple_of(start + j * BLOCK, BLOCK)
            even = iota((BLOCK, LANES), 0) % 2 == 0
            values = [opp[b, v, pl.ds(r0, BLOCK), :] for b in range(modes)]
            values = [jnp.where(even, x, -x) for x in values]
            for a in range(modes):
                total = res[a, v, pl.ds(r0, BLOCK), :]
                mate = partner[a] % modes
                for b in range(modes):
                    total = total + values[b] * jnp.where(mate == b, 1.0, 0.0)
                sens[a, v, pl.ds(r0, BLOCK), :] = total

    @pl.loop(0, chunks)
    def _(q):
        beside(q).wait_send()
        onward(q).wait_send()


def per_device(
    adjoint,
    source,
    derivative,
    lift_matrix,
    jacobian,
    harmonics,
    swirl_rate,
    coupling,
    mode_number,
    partner,
    upstream,
    face_list,
):
    modes, _, nv, cells = adjoint.shape
    face_count = face_list.shape[0]
    tiles = cells // LANES
    rows = 2 * tiles
    frows = face_count

    def to_rows(x):
        x = x.reshape(modes, 2, nv, tiles, LANES)
        return x.transpose(0, 2, 3, 1, 4).reshape(modes, nv, rows, LANES)

    def from_rows(x):
        x = x.reshape(modes, nv, tiles, 2, LANES)
        return x.transpose(0, 3, 1, 2, 4).reshape(modes, 2, nv, cells)

    panel = (modes, nv, rows, LANES)
    small = (modes, nv, frows, LANES)
    smem = pl.BlockSpec(memory_space=pltpu.SMEM)
    vmem = pl.BlockSpec(memory_space=pltpu.VMEM)
    hbm = pl.BlockSpec(memory_space=pl.ANY)
    residual, sensitivity = pl.pallas_call(
        kernel,
        out_shape=[jax.ShapeDtypeStruct(panel, jnp.float32)] * 2,
        in_specs=[smem] * 4 + [hbm] * 2 + [vmem] * 6,
        out_specs=[vmem] * 2,
        scratch_shapes=[
            pltpu.VMEM(panel, jnp.float32),
            pltpu.VMEM(panel, jnp.float32),
            pltpu.VMEM((4,) + panel, jnp.float32),
            pltpu.VMEM(panel, jnp.float32),
            pltpu.VMEM(panel, jnp.float32),
            pltpu.VMEM(small, jnp.float32),
            pltpu.VMEM(small, jnp.float32),
            pltpu.VMEM((3 * LANES, LANES), jnp.float32),
            pltpu.VMEM((2 * rows + 2 * frows, 2 * rows), jnp.bfloat16),
            pltpu.VMEM((2 * rows, 2 * frows), jnp.bfloat16),
            pltpu.VMEM((TAPS, rows, LANES), jnp.float32),
            pltpu.VMEM((rows, LANES), jnp.float32),
            pltpu.SemaphoreType.DMA((5, 2 * nv)),
            pltpu.SemaphoreType.DMA((5, 2 * nv)),
            pltpu.SemaphoreType.DMA((2,)),
            pltpu.SemaphoreType.DMA((2,)),
        ],
        compiler_params=pltpu.CompilerParams(
            collective_id=0, has_side_effects=True, vmem_limit_bytes=60 * 1024 * 1024
        ),
    )(
        coupling.transpose(0, 2, 3, 1).reshape(modes * 2 * modes, TAPS),
        jacobian,
        mode_number,
        partner,
        to_rows(adjoint),
        to_rows(source),
        derivative,
        lift_matrix,
        upstream.reshape(1, -1),
        face_list.reshape(1, -1),
        harmonics.reshape(TAPS, tiles, LANES).transpose(1, 0, 2),
        swirl_rate.reshape(tiles, LANES),
    )
    return (from_rows(residual), from_rows(sensitivity))


def solution(mesh):
    in_specs = (
        P("mode", None, None, "slab"),
        P("mode", None, None, "slab"),
        P(),
        P(),
        P(),
        P(None, "slab"),
        P("slab"),
        P("mode", None, None, None),
        P("mode"),
        P("mode"),
        P("slab"),
        P("slab"),
    )
    out_specs = (P("mode", None, None, "slab"), P("mode", None, None, "slab"))
    return jax.shard_map(
        per_device, mesh=mesh, in_specs=in_specs, out_specs=out_specs, check_vma=False
    )
```

```python
import jax
import jax.numpy as jnp
from jax import lax
from jax.experimental import pallas as pl
from jax.experimental.pallas import tpu as pltpu
from jax.sharding import PartitionSpec as P

TAPS = 5
BLOCK = 32
LANES = 128
WINDOW = 3
MESH = pl.DeviceIdType.MESH


def split(x):
    high = x.astype(jnp.bfloat16)
    low = (x - high.astype(jnp.float32)).astype(jnp.bfloat16)
    return high, low


def dot(a, b):
    return jnp.dot(a, b, preferred_element_type=jnp.float32)


def dot_t(a, b):
    return lax.dot_general(a, b, (((1,), (1,)), ((), ())), preferred_element_type=jnp.float32)


def times_i(x):
    even = lax.broadcasted_iota(jnp.int32, x.shape, 0) % 2 == 0
    return jnp.where(even, -pltpu.roll(x, x.shape[0] - 1, 0), pltpu.roll(x, 1, 0))


def doubled(x, half):
    low = lax.broadcasted_iota(jnp.int32, x.shape, 1) < LANES // 2
    other = pltpu.roll(x, LANES // 2, 1)
    return jnp.where(low, x, other) if half == 0 else jnp.where(low, other, x)


def by_half(x, y):
    return jnp.where(lax.broadcasted_iota(jnp.int32, x.shape, 1) < LANES // 2, x, y)


def spot(i, span):
    return (i % span) // 2 * 2 + i // span


def kernel(
    coup,
    jac,
    number,
    partner,
    adj_hbm,
    src_hbm,
    derivative,
    lift,
    upstream,
    face_list,
    harm_in,
    swirl_in,
    res_hbm,
    sens_hbm,
    res,
    sens,
    adj,
    src,
    near,
    opp,
    mer,
    faces,
    halo,
    kmat,
    pick,
    pick_halo,
    harm,
    swirl,
    send_sem,
    recv_sem,
    halo_sem,
    load_sem,
    save_sem,
):
    modes, nv, rows, _ = adj.shape
    chunks = 2 * nv
    part = rows // 2
    frows = faces.shape[2]
    n_mode = lax.axis_size("mode")
    n_slab = lax.axis_size("slab")
    me = lax.axis_index("mode")
    slab = lax.axis_index("slab")
    odd = me % 2
    above = (me + 2) % n_mode
    below = (me + n_mode - 2) % n_mode
    pair = me + 1 - 2 * odd
    across = (me + n_mode // 2) % n_mode
    after = (slab + 1) % n_slab
    before = (slab + n_slab - 1) % n_slab

    load_adj = pltpu.make_async_copy(adj_hbm, adj, load_sem.at[0])
    load_src = pltpu.make_async_copy(src_hbm, src, load_sem.at[1])
    load_adj.start()
    load_src.start()

    barrier = pltpu.get_barrier_semaphore()
    for other in (above, below, pair, across):
        pl.semaphore_signal(barrier, inc=1, device_id=(other, slab), device_id_type=MESH)
    for other in (after, before):
        pl.semaphore_signal(barrier, inc=1, device_id=(me, other), device_id_type=MESH)
    pl.semaphore_wait(barrier, 6)
    load_adj.wait()

    def place(q):
        return q // 2, pl.multiple_of(q % 2 * part, part)

    def copy(kind, q, source, target, device):
        v, r0 = place(q)
        return pltpu.make_async_remote_copy(
            src_ref=source.at[:, v, pl.ds(r0, part)],
            dst_ref=target.at[:, v, pl.ds(r0, part)],
            send_sem=send_sem.at[kind, q],
            recv_sem=recv_sem.at[kind, q],
            device_id=(device, slab),
            device_id_type=MESH,
        )

    def up(q):
        return copy(0, q, adj, near.at[0], above)

    def down(q):
        return copy(1, q, adj, near.at[1], below)

    def beside(q):
        return copy(2, q, adj, near.at[2], pair)

    def onward(q):
        return copy(3, q, near.at[1 - odd], near.at[3], pair)

    def over(q):
        return copy(4, q, res, opp, across)

    def save(kind, q):
        v, r0 = place(q)
        return pltpu.make_async_copy(
            (res, sens)[kind].at[:, v, pl.ds(r0, part)],
            (res_hbm, sens_hbm)[kind].at[:, v, pl.ds(r0, part)],
            save_sem.at[kind, q],
        )

    def begin(q):
        up(q).start()
        down(q).start()
        beside(q).start()

    @pl.loop(0, WINDOW)
    def _(q):
        begin(q)

    def arrive(q):
        up(q).wait_send()
        down(q).wait_send()

        @pl.when(q + WINDOW < chunks)
        def _():
            begin(q + WINDOW)

        up(q).wait_recv()
        down(q).wait_recv()
        onward(q).start()
        beside(q).wait_recv()

    span = rows
    d = derivative[...]
    low = lift[...]
    none = jnp.zeros_like(d)
    kmat[...] = jnp.concatenate(
        [
            jnp.concatenate([d, none], axis=1),
            jnp.concatenate([none, d], axis=1),
            jnp.concatenate([low, none], axis=1),
            jnp.concatenate([low, none], axis=1),
            jnp.concatenate([none, low], axis=1),
            jnp.concatenate([none, low], axis=1),
        ],
        axis=0,
    )

    def iota(shape, axis):
        return lax.broadcasted_iota(jnp.int32, shape, axis)

    def wanted_rows(values, count, span_out):
        held = values.shape[1]
        mine = spot(iota((count, held), 0), span_out)
        chosen = jnp.where(mine == iota((count, held), 1), values, 0.0)
        return jnp.sum(chosen, axis=1, keepdims=True)

    def one_hot(wanted, count, width, span_in):
        held = spot(iota((count, width), 1), span_in).astype(jnp.float32)
        same = (iota((count, width), 0) % 2) == (iota((count, width), 1) % 2)
        hot = jnp.where(wanted == held, 1.0, 0.0)
        return jnp.where(same, hot, 0.0).astype(jnp.bfloat16)

    source_row = wanted_rows(upstream[...].astype(jnp.float32), 2 * rows, span)
    face_row = wanted_rows(face_list[...].astype(jnp.float32), 2 * frows, frows)
    pick[: 2 * rows] = one_hot(source_row - float(frows), 2 * rows, 2 * rows, span)
    pick[2 * rows :] = one_hot(face_row, 2 * frows, 2 * rows, span)
    pick_halo[...] = one_hot(source_row, 2 * rows, 2 * frows, frows)

    twice = jnp.where(
        iota((rows, rows // 2), 0) // 2 == iota((rows, rows // 2), 1), 1.0, 0.0
    ).astype(jnp.bfloat16)

    def double(x):
        high = x.astype(jnp.bfloat16)
        rest, last = split(x - high.astype(jnp.float32))
        return dot(twice, high) + dot(twice, rest) + dot(twice, last)

    for tap in range(TAPS):
        harm[tap] = double(harm_in[:, tap, :])
    swirl[...] = double(swirl_in[...])
    load_src.wait()

    half_modes = float(modes * n_mode // 2)
    fac = [number[a].astype(jnp.float32) / half_modes for a in range(modes)]

    def gather(i):
        m = i // nv
        v = i % nv
        k_high, k_low = split(kmat[...])
        x_high, x_low = split(adj[m, v])
        lifted = dot_t(x_high, k_high) + dot_t(x_low, k_high) + dot_t(x_high, k_low)
        tall = jnp.concatenate([lifted[:, LANES : 2 * LANES], lifted[:, 2 * LANES :]], axis=0)
        picked = dot(pick[...], jnp.concatenate(split(tall), axis=1))
        picked = picked[:, :LANES] + picked[:, LANES:]
        mer[m, v] = lifted[:, :LANES] + by_half(picked[:rows], picked[rows : 2 * rows])
        faces[m, v] = by_half(
            picked[2 * rows : 2 * rows + frows], picked[2 * rows + frows :]
        )

    halo_copy = pltpu.make_async_remote_copy(
        src_ref=faces,
        dst_ref=halo,
        send_sem=halo_sem.at[0],
        recv_sem=halo_sem.at[1],
        device_id=(me, after),
        device_id_type=MESH,
    )

    def mix(total, values, tap, r0):
        turned = [times_i(x) for x in values]
        amplitude = harm[tap, pl.ds(r0, BLOCK), :]
        out = []
        for a in range(modes):
            at = a * 2 * modes
            term = values[0] * coup[at, tap] + turned[0] * coup[at + modes, tap]
            for b in range(1, modes):
                term = term + values[b] * coup[at + b, tap]
                term = term + turned[b] * coup[at + modes + b, tap]
            out.append(total[a] - term * amplitude)
        return out

    def direct(q):
        v, start = place(q)

        @pl.loop(0, part // BLOCK)
        def _(j):
            r0 = pl.multiple_of(start + j * BLOCK, BLOCK)
            values = [adj[b, v, pl.ds(r0, BLOCK), :] for b in range(modes)]
            rate = swirl[pl.ds(r0, BLOCK), :]
            total = [
                src[a, v, pl.ds(r0, BLOCK), :] - times_i(values[a]) * (rate * fac[a])
                for a in range(modes)
            ]
            total = mix(total, values, TAPS // 2, r0)
            for slot, tap in ((0, 4), (1, 0), (2, 1 + 2 * odd)):
                values = [near[slot, b, v, pl.ds(r0, BLOCK), :] for b in range(modes)]
                total = mix(total, values, tap, r0)
            for a in range(modes):
                res[a, v, pl.ds(r0, BLOCK), :] = total[a]

    def finish(q):
        onward(q).wait_recv()
        v, start = place(q)

        @pl.loop(0, part // BLOCK)
        def _(j):
            r0 = pl.multiple_of(start + j * BLOCK, BLOCK)
            total = []
            for a in range(modes):
                term = res[a, v, pl.ds(r0, BLOCK), :]
                for w in range(nv):
                    term = term - mer[a, w, pl.ds(r0, BLOCK), :] * jac[v, w]
                total.append(term)
            values = [near[3, b, v, pl.ds(r0, BLOCK), :] for b in range(modes)]
            total = mix(total, values, 3 - 2 * odd, r0)
            for a in range(modes):
                res[a, v, pl.ds(r0, BLOCK), :] = total[a]

        save(0, q).start()

    @pl.loop(0, nv)
    def _(q):
        @pl.loop(q * modes, (q + 1) * modes)
        def _(i):
            gather(i)

        arrive(q)
        direct(q)

    halo_copy.start()

    @pl.loop(nv, nv + 1)
    def _(q):
        arrive(q)
        direct(q)

    halo_copy.wait()
    present = jnp.where(slab == 0, 0.0, 1.0)

    @pl.loop(0, modes * nv)
    def _(i):
        m = i // nv
        v = i % nv
        got = halo[m, v] * present
        tall = jnp.concatenate([doubled(got, 0), doubled(got, 1)], axis=0)
        picked = dot(pick_halo[...], jnp.concatenate(split(tall), axis=1))
        picked = picked[:, :LANES] + picked[:, LANES:]
        mer[m, v] = mer[m, v] + by_half(picked[:rows], picked[rows:])

    @pl.loop(nv + 1, chunks)
    def _(q):
        @pl.when(q == chunks - 1)
        def _():
            over(0).start()

        arrive(q)
        direct(q)

        @pl.loop(2 * (q - nv - 1), 2 * (q - nv))
        def _(c):
            finish(c)

    @pl.loop(1, WINDOW)
    def _(q):
        over(q).start()

    @pl.loop(2 * (nv - 1), chunks)
    def _(q):
        finish(q)

    @pl.loop(0, chunks)
    def _(q):
        over(q).wait_send()

        @pl.when(q + WINDOW < chunks)
        def _():
            over(q + WINDOW).start()

        over(q).wait_recv()
        v, start = place(q)

        @pl.loop(0, part // BLOCK)
        def _(j):
            r0 = pl.multiple_of(start + j * BLOCK, BLOCK)
            even = iota((BLOCK, LANES), 0) % 2 == 0
            values = [opp[b, v, pl.ds(r0, BLOCK), :] for b in range(modes)]
            values = [jnp.where(even, x, -x) for x in values]
            for a in range(modes):
                total = res[a, v, pl.ds(r0, BLOCK), :]
                mate = partner[a] % modes
                for b in range(modes):
                    total = total + values[b] * jnp.where(mate == b, 1.0, 0.0)
                sens[a, v, pl.ds(r0, BLOCK), :] = total

        save(1, q).start()

    @pl.loop(0, chunks)
    def _(q):
        beside(q).wait_send()
        onward(q).wait_send()
        save(0, q).wait()
        save(1, q).wait()


def per_device(
    adjoint,
    source,
    derivative,
    lift_matrix,
    jacobian,
    harmonics,
    swirl_rate,
    coupling,
    mode_number,
    partner,
    upstream,
    face_list,
):
    modes, _, nv, cells = adjoint.shape
    face_count = face_list.shape[0]
    tiles = cells // LANES
    rows = 2 * tiles
    frows = face_count

    def to_rows(x):
        x = x.reshape(modes, 2, nv, tiles, LANES)
        return x.transpose(0, 2, 3, 1, 4).reshape(modes, nv, rows, LANES)

    def from_rows(x):
        x = x.reshape(modes, nv, tiles, 2, LANES)
        return x.transpose(0, 3, 1, 2, 4).reshape(modes, 2, nv, cells)

    panel = (modes, nv, rows, LANES)
    small = (modes, nv, frows, LANES)
    smem = pl.BlockSpec(memory_space=pltpu.SMEM)
    vmem = pl.BlockSpec(memory_space=pltpu.VMEM)
    hbm = pl.BlockSpec(memory_space=pl.ANY)
    residual, sensitivity = pl.pallas_call(
        kernel,
        out_shape=[jax.ShapeDtypeStruct(panel, jnp.float32)] * 2,
        in_specs=[smem] * 4 + [hbm] * 2 + [vmem] * 6,
        out_specs=[hbm] * 2,
        scratch_shapes=[
            pltpu.VMEM(panel, jnp.float32),
            pltpu.VMEM(panel, jnp.float32),
            pltpu.VMEM(panel, jnp.float32),
            pltpu.VMEM(panel, jnp.float32),
            pltpu.VMEM((4,) + panel, jnp.float32),
            pltpu.VMEM(panel, jnp.float32),
            pltpu.VMEM(panel, jnp.float32),
            pltpu.VMEM(small, jnp.float32),
            pltpu.VMEM(small, jnp.float32),
            pltpu.VMEM((3 * LANES, LANES), jnp.float32),
            pltpu.VMEM((2 * rows + 2 * frows, 2 * rows), jnp.bfloat16),
            pltpu.VMEM((2 * rows, 2 * frows), jnp.bfloat16),
            pltpu.VMEM((TAPS, rows, LANES), jnp.float32),
            pltpu.VMEM((rows, LANES), jnp.float32),
            pltpu.SemaphoreType.DMA((5, 2 * nv)),
            pltpu.SemaphoreType.DMA((5, 2 * nv)),
            pltpu.SemaphoreType.DMA((2,)),
            pltpu.SemaphoreType.DMA((2,)),
            pltpu.SemaphoreType.DMA((2, 2 * nv)),
        ],
        compiler_params=pltpu.CompilerParams(
            collective_id=0, has_side_effects=True, vmem_limit_bytes=60 * 1024 * 1024
        ),
    )(
        coupling.transpose(0, 2, 3, 1).reshape(modes * 2 * modes, TAPS),
        jacobian,
        mode_number,
        partner,
        to_rows(adjoint),
        to_rows(source),
        derivative,
        lift_matrix,
        upstream.reshape(1, -1),
        face_list.reshape(1, -1),
        harmonics.reshape(TAPS, tiles, LANES).transpose(1, 0, 2),
        swirl_rate.reshape(tiles, LANES),
    )
    return (from_rows(residual), from_rows(sensitivity))


def solution(mesh):
    in_specs = (
        P("mode", None, None, "slab"),
        P("mode", None, None, "slab"),
        P(),
        P(),
        P(),
        P(None, "slab"),
        P("slab"),
        P("mode", None, None, None),
        P("mode"),
        P("mode"),
        P("slab"),
        P("slab"),
    )
    out_specs = (P("mode", None, None, "slab"), P("mode", None, None, "slab"))
    return jax.shard_map(
        per_device, mesh=mesh, in_specs=in_specs, out_specs=out_specs, check_vma=False
    )
```
